32 devices in a mesh: grp: 4 (over x, core), row: 8 (over z, y).
Axes of the slice: x: 2, y: 2, z: 4, core: 2. Of those that a mesh axis runs over, the one named last changes fastest.
Arguments:
- users: bfloat16 [4096, 512], P(('grp', 'row')), may hold values from -0.44921875 to 0.44921875
- items: bfloat16 [6144, 512], P('row'), may hold values from -0.8984375 to 0.8984375
- ratings: float32 [32, 16, 128, 128], P(('grp', 'row')), may hold values from 0.05 to 1
- pair_list: int32 [32, 16, 2], P(('grp', 'row')), may hold values from 0 to 15, as said below
- send_list: int32 [32, 8, 2], P(('grp', 'row')), may hold values from 0 to 5, as said below
- counts: int32 [32], P(('grp', 'row')), may hold values from 4 to 16
Outputs:
- new_users: float32 [4096, 512], P(('grp', 'row'))
- new_items: float32 [6144, 512], P('row')
The draws below stay inside these ranges and needn't reach their ends.
Inputs may be any that keep to these rules, and one draw needn't show every extreme that they name: pair_list[d, i, 0] is below 1 and pair_list[d, i, 1] below 8 * 2; the first counts[d] pairs of a device are distinct. The 2 entries send_list[d, p, :] are distinct.
All inputs are finite; a program needn't handle non-finite values.
Results may differ from the reference program's by a relative error of at most 0.0027.
Values may be sent and summed in bfloat16 or wider, within the bound.
No kernel may reach another device: no remote copies, remote signals or barrier semaphores. Data moves between devices by JAX's collectives and lax.ppermute only.
A program may use at most 64 MiB of HBM per device.

```python
import math
import jax
import jax.numpy as jnp
from jax import lax

K = 512
BLK = 128
UB_DEV = 1
IB_DEV = 6
SEND_LIMIT = 2
OBS_DEV = 16
USERS = 4096
ITEMS = 6144
N_GRP = 4
N_ROW = 8
DEVICES = 32


def draw_send_list(key, part):
    key = jax.random.fold_in(key, 3)
    scores = jax.random.randint(key, (N_GRP, N_ROW, N_ROW, IB_DEV), 0, 65536) * IB_DEV
    scores = scores + jnp.arange(IB_DEV, dtype=jnp.int32)
    order = jnp.argsort(scores, axis=-1, stable=True)[..., :SEND_LIMIT].astype(jnp.int32)
    return jnp.transpose(order, (0, 2, 1, 3)).reshape(DEVICES, N_ROW, SEND_LIMIT)


def draw_pair_list(key, part):
    key = jax.random.fold_in(key, 7)
    combos = UB_DEV * N_ROW * SEND_LIMIT
    scores = jax.random.randint(key, (DEVICES, combos), 0, 65536) * combos
    scores = scores + jnp.arange(combos, dtype=jnp.int32)
    picked = jnp.argsort(scores, axis=-1, stable=True)[:, :OBS_DEV].astype(jnp.int32)
    user_part = picked // (N_ROW * SEND_LIMIT)
    slot_part = picked % (N_ROW * SEND_LIMIT)
    return jnp.stack([user_part, slot_part], axis=-1).astype(jnp.int32)


def draw_counts(key, part):
    key = jax.random.fold_in(key, 11)
    first, second = jax.random.split(key)
    shifts = jax.random.randint(first, (DEVICES,), 0, 3)
    values = OBS_DEV // jnp.left_shift(jnp.ones_like(shifts), shifts)
    busiest = jax.random.randint(second, (), 0, DEVICES)
    values = jnp.where(jnp.arange(DEVICES, dtype=jnp.int32) == busiest, OBS_DEV, values)
    return values.astype(jnp.int32)


def levels(stream_key, dims, cuts, low, top_value):
    level, own = 1.0, jax.random.fold_in(stream_key, 6)
    for axis_at, blocks in cuts:
        steps = jnp.exp(jax.random.uniform(jax.random.fold_in(own, axis_at), (blocks,), jnp.float32, low / len(cuts), top_value / len(cuts)))
        level = level * jnp.repeat(steps, dims[axis_at] // blocks).reshape([-1 if axis == axis_at else 1 for axis in range(len(dims))])
    return level


def gaussian(stream_key, shape, deviation, limit, cuts=(), kind=jnp.bfloat16):
    drawn = deviation * jax.random.normal(stream_key, shape, jnp.float32)
    if cuts:
        drawn = drawn * levels(stream_key, shape, cuts, -0.22, 0.18)
    return jnp.clip(drawn, -limit, limit).astype(kind)


def setup_inputs(seed: int = 0) -> dict:
    splits = jax.random.split(jax.random.key(seed), 7)
    return {
        "users": gaussian(splits[0], (USERS, K), 0.075, 0.44921875, ((0, 32),)),
        "items": gaussian(splits[1], (ITEMS, K), 0.15, 0.8984375, ((0, 8),)),
        "ratings": jnp.clip(jnp.exp(math.log(1.0) - 2.9957323 * jax.random.uniform(splits[2], (DEVICES, OBS_DEV, BLK, BLK), jnp.float32) ** levels(splits[2], (DEVICES, OBS_DEV, BLK, BLK), ((0, 32),), -0.2, 0.2)), 0.05, 1.0),
        "pair_list": draw_pair_list(jax.random.fold_in(splits[6], 71), 0),
        "send_list": draw_send_list(jax.random.fold_in(splits[6], 71), 0),
        "counts": draw_counts(jax.random.fold_in(splits[6], 71), 0),
    }


CONFIDENCE = 40.0
FULL = lax.Precision.HIGHEST

def reference(users, items, ratings, pair_list, send_list, counts):
    contract = (((0,), (0,)), ((), ()))
    item_gram = lax.dot_general(items, items, contract, preferred_element_type=jnp.float32)
    user_gram = lax.dot_general(users, users, contract, preferred_element_type=jnp.float32)
    item_blocks = items.reshape(IB_DEV * N_ROW, BLK, K)
    user_blocks = users.reshape(DEVICES, UB_DEV, BLK, K)
    position_count = N_ROW * SEND_LIMIT

    def device_step(carry, inputs):
        blocks, rates, pairs, count, device = inputs
        group = device // N_ROW
        row_pos = device % N_ROW
        table = lax.dynamic_slice_in_dim(send_list, (group * N_ROW).astype(jnp.int32), N_ROW, 0)
        mine = jnp.take(table, row_pos, axis=1)
        slot_item = (mine + IB_DEV * jnp.arange(N_ROW, dtype=jnp.int32)[:, None]).reshape(-1)
        user_idx = pairs[:, 0]
        position_index = pairs[:, 1]
        lefts = jnp.take(blocks, user_idx, axis=0).astype(jnp.float32)
        rights = jnp.take(item_blocks, jnp.take(slot_item, position_index), axis=0).astype(jnp.float32)
        scores = jnp.einsum('obk,ock->obc', lefts, rights, precision=FULL)
        live = jnp.arange(OBS_DEV, dtype=jnp.int32) < count
        weighted = CONFIDENCE * rates
        errors = jnp.where(live[:, None, None], weighted * scores - 1.0 - weighted, 0.0)
        errors = lax.optimization_barrier(errors.astype(jnp.bfloat16)).astype(jnp.float32)
        user_terms = jnp.einsum('obc,ock->obk', errors, rights, precision=FULL)
        user_hot = (user_idx[:, None] == jnp.arange(UB_DEV, dtype=jnp.int32)[None, :]).astype(jnp.float32)
        user_acc = jnp.einsum('ou,obk->ubk', user_hot, user_terms, precision=FULL)
        slot_terms = jnp.einsum('obc,obk->ock', errors, lefts, precision=FULL)
        position_onehot = (position_index[:, None] == jnp.arange(position_count, dtype=jnp.int32)[None, :]).astype(jnp.float32)
        slot_sum = jnp.einsum('os,ock->sck', position_onehot, slot_terms, precision=FULL)
        slot_sum = lax.optimization_barrier(slot_sum.astype(jnp.bfloat16)).astype(jnp.float32)
        item_hot = (slot_item[:, None] == jnp.arange(IB_DEV * N_ROW, dtype=jnp.int32)[None, :]).astype(jnp.float32)
        carry = carry + jnp.einsum('si,sck->ick', item_hot, slot_sum, precision=FULL)
        return (carry, user_acc)
    start = jnp.zeros((IB_DEV * N_ROW, BLK, K), jnp.float32)
    device_ids = jnp.arange(DEVICES, dtype=jnp.int32)
    item_terms, user_terms = lax.scan(device_step, start, (user_blocks, ratings, pair_list, counts, device_ids))
    users_full = users.astype(jnp.float32)
    items_full = items.astype(jnp.float32)
    grad_users = jnp.dot(users_full, item_gram, precision=FULL) + user_terms.reshape(-1, K)
    grad_items = jnp.dot(items_full, user_gram, precision=FULL) + item_terms.reshape(-1, K)
    new_users = users_full - 4.0 / jnp.sqrt(jnp.float32(ITEMS)) * grad_users
    new_items = items_full - 8.0 / jnp.sqrt(jnp.float32(USERS)) * grad_items
    return (new_users, new_items)
```

```python
import functools
import math

import jax
import jax.numpy as jnp
from jax import lax
from jax.experimental import pallas as pl
from jax.experimental.pallas import tpu as pltpu
from jax.sharding import PartitionSpec as P

CONFIDENCE = 40.0
STEPS = 65535.0
OFFSET = 32768
BF = jnp.bfloat16
F32 = jnp.float32

VM = pl.BlockSpec(memory_space=pltpu.VMEM)
SM = pl.BlockSpec(memory_space=pltpu.SMEM)
ROWS = (((1,), (1,)), ((), ()))
COLS = (((0,), (0,)), ((), ()))


def call(body, outs, in_specs, flops, moved, scratch=(), mib=24):
    return pl.pallas_call(
        body,
        out_shape=outs,
        in_specs=in_specs,
        out_specs=jax.tree.map(lambda _: VM, outs),
        scratch_shapes=scratch,
        compiler_params=pltpu.CompilerParams(vmem_limit_bytes=mib << 20),
        cost_estimate=pl.CostEstimate(flops=flops, bytes_accessed=moved, transcendentals=0),
    )


def spread_body(n, limit, pair_ref, count_ref, rate_ref, *rest):
    outs, where = rest[:n], rest[n]
    me = lax.axis_index("row")
    width = rate_ref.shape[1]
    for s in range(n * limit):
        where[s] = -1
    for i in range(rate_ref.shape[0]):
        @pl.when(i < count_ref[0])
        def _():
            where[pair_ref[1, i]] = i
    for k in range(n):
        for c in range(limit):
            i = where[(me ^ k) * limit + c]
            rate = rate_ref[jnp.maximum(i, 0)]
            code = jnp.where(i >= 0, (rate * STEPS + 0.5).astype(jnp.int32), 0) - OFFSET
            outs[k][c * width : (c + 1) * width] = code.astype(jnp.int16)


def gram_body(item_ref, gram_ref):
    items = item_ref[...]
    gram_ref[...] = lax.dot_general(items, items, COLS, preferred_element_type=F32).astype(BF)


def score_body(n, limit, width, send_ref, item_ref, gram_ref, *rest):
    users, (score_ref, user_ref, part_ref) = rest[:n], rest[n:]
    me = lax.axis_index("row")
    gram = gram_ref[...]
    total = None
    for k in range(n):
        left = users[k][...]
        for c in range(limit):
            at = pl.multiple_of(send_ref[c, me ^ k] * width, width)
            score_ref[k * limit + c] = lax.dot_general(
                left, item_ref[pl.ds(at, width)], ROWS, preferred_element_type=F32
            )
        user_ref[k] = jnp.dot(left, gram, preferred_element_type=F32)
        term = lax.dot_general(left, left, COLS, preferred_element_type=F32)
        total = term if total is None else total + term
    part_ref[...] = jnp.dot(item_ref[...], total.astype(BF), preferred_element_type=F32)


def error_body(n, limit, width, send_ref, item_ref, score_ref, gram_user_ref, part_ref, *rest):
    users, codes, outs = rest[:n], rest[n : 2 * n], rest[2 * n : 3 * n]
    mine_ref, other_ref, sum_ref = rest[3 * n :]
    me = lax.axis_index("row")
    core = lax.axis_index("grp") % 2
    sum_ref[...] = part_ref[...]
    for k in range(n):
        left = users[k][...]
        total = gram_user_ref[k]
        for c in range(limit):
            at = pl.ds(pl.multiple_of(send_ref[c, me ^ k] * width, width), width)
            code = codes[k][c * width : (c + 1) * width].astype(jnp.int32) + OFFSET
            weighted = CONFIDENCE * (code.astype(F32) * (1.0 / STEPS))
            error = weighted * score_ref[k * limit + c] - 1.0 - weighted
            error = jnp.where(code > 0, error, 0.0).astype(BF)
            total += jnp.dot(error, item_ref[at], preferred_element_type=F32)
            term = lax.dot_general(error, left, COLS, preferred_element_type=F32)
            sum_ref[at] += term.astype(BF).astype(F32)
        outs[k][...] = total.astype(outs[k].dtype)
    half = mine_ref.shape[0]
    mine_ref[...] = sum_ref[pl.ds(pl.multiple_of(core * half, half), half)]
    other_ref[...] = sum_ref[pl.ds(pl.multiple_of((1 - core) * half, half), half)].astype(BF)


def swap(x, axis, k):
    return lax.ppermute(x, axis, [(i, i ^ k) for i in range(lax.axis_size(axis))])


def shards(users, items, ratings, pair_list, send_list, counts):
    n = lax.axis_size("row")
    grp_n = lax.axis_size("grp")
    width = ratings.shape[2]
    factors = users.shape[1]
    limit = send_list.shape[2]
    item_rows = items.shape[0]
    user_rows = users.shape[0]
    far = n // 2
    total_users = user_rows * grp_n * n
    total_items = item_rows * n
    sds = jax.ShapeDtypeStruct

    pairs = jnp.swapaxes(pair_list[0], 0, 1)
    sends = jnp.swapaxes(send_list[0], 0, 1)

    over = swap(users, "row", far)
    blocks = [users] + [swap(users, "row", k) for k in range(1, far)]
    blocks += [over] + [swap(over, "row", k) for k in range(1, far)]

    codes = call(
        functools.partial(spread_body, n, limit),
        [sds((limit * width, width), jnp.int16)] * n,
        [SM, SM, VM],
        0,
        ratings.size * 6,
        [pltpu.SMEM((n * limit,), jnp.int32)],
    )(pairs, counts, ratings[0])
    codes = [codes[0]] + [swap(codes[k], "row", k) for k in range(1, n)]

    gram = call(
        gram_body, sds((factors, factors), BF), [VM], 2 * item_rows * factors**2, items.size * 2
    )(items)
    scores, user_gram, item_part = call(
        functools.partial(score_body, n, limit, width),
        [
            sds((n * limit, user_rows, width), F32),
            sds((n, user_rows, factors), F32),
            sds((item_rows, factors), F32),
        ],
        [SM, VM, VM] + [VM] * n,
        2 * n * user_rows * factors * (limit * width + 2 * factors) + 2 * item_rows * factors**2,
        8 << 20,
    )(sends, items, gram, *blocks)
    half = item_rows // 2
    *parts, mine, other = call(
        functools.partial(error_body, n, limit, width),
        [sds((user_rows, factors), F32 if k in (0, far) else BF) for k in range(n)]
        + [sds((half, factors), F32), sds((half, factors), BF)],
        [SM, VM, VM, VM, VM] + [VM] * (2 * n),
        4 * n * limit * user_rows * factors * width,
        8 << 20,
        [pltpu.VMEM((item_rows, factors), F32)],
    )(sends, items, scores, user_gram, item_part, *blocks, *codes)

    across = parts[far]
    for k in range(1, far):
        across += swap(parts[far + k], "row", k).astype(F32)
    user_sum = parts[0]
    for k in range(1, far):
        user_sum += swap(parts[k], "row", k).astype(F32)
    user_sum += swap(across.astype(BF), "row", far).astype(F32)
    new_users = users.astype(F32) - 4.0 / math.sqrt(total_items) * user_sum

    core = lax.axis_index("grp") % 2
    pair_sum = mine + swap(other, "grp", 1).astype(F32)
    if grp_n == 4:
        here = pair_sum.astype(BF)
        there = swap(here, "grp", 2)
        first = here.astype(F32) + there.astype(F32)
        second = swap(here, "grp", 1).astype(F32) + swap(there, "grp", 1).astype(F32)
    else:
        peers = [list(range(c, grp_n, 2)) for c in range(2)]
        first = lax.psum(pair_sum, "grp", axis_index_groups=peers)
        second = swap(first, "grp", 1)
    item_sum = jnp.where(
        core == 0, jnp.concatenate([first, second]), jnp.concatenate([second, first])
    )
    new_items = items.astype(F32) - 8.0 / math.sqrt(total_users) * item_sum
    return (new_users, new_items)


def solution(mesh):
    in_specs = (
        P(("grp", "row"), None),
        P("row", None),
        P(("grp", "row"), None, None, None),
        P(("grp", "row"), None, None),
        P(("grp", "row"), None, None),
        P(("grp", "row")),
    )
    out_specs = (P(("grp", "row"), None), P("row", None))
    return jax.shard_map(shards, mesh=mesh, in_specs=in_specs, out_specs=out_specs, check_vma=False)
```

```python
import functools
import math

import jax
import jax.numpy as jnp
from jax import lax
from jax.experimental import pallas as pl
from jax.experimental.pallas import tpu as pltpu
from jax.sharding import PartitionSpec as P

CONFIDENCE = 40.0
STEPS = 65535.0
OFFSET = 32768
BF = jnp.bfloat16
F32 = jnp.float32

VM = pl.BlockSpec(memory_space=pltpu.VMEM)
SM = pl.BlockSpec(memory_space=pltpu.SMEM)
ROWS = (((1,), (1,)), ((), ()))
COLS = (((0,), (0,)), ((), ()))


def call(body, outs, in_specs, flops, moved, scratch=(), mib=24):
    return pl.pallas_call(
        body,
        out_shape=outs,
        in_specs=in_specs,
        out_specs=jax.tree.map(lambda _: VM, outs),
        scratch_shapes=scratch,
        compiler_params=pltpu.CompilerParams(vmem_limit_bytes=mib << 20),
        cost_estimate=pl.CostEstimate(flops=flops, bytes_accessed=moved, transcendentals=0),
    )


def slots(n, limit, pair_ref, count_ref, where):
    for s in range(n * limit):
        where[s] = -1
    for i in range(pair_ref.shape[1]):
        @pl.when(i < count_ref[0])
        def _():
            where[pair_ref[1, i]] = i


def coded(limit, rate_ref, where, peer, c):
    i = where[peer * limit + c]
    rate = rate_ref[jnp.maximum(i, 0)]
    code = jnp.where(i >= 0, (rate * STEPS + 0.5).astype(jnp.int32), 0) - OFFSET
    return code.astype(jnp.int16)


def give_body(n, limit, pair_ref, count_ref, rate_ref, out_ref, where):
    slots(n, limit, pair_ref, count_ref, where)
    me, far, width = lax.axis_index("row"), n // 2, rate_ref.shape[1]
    first = far * (1 - lax.axis_index("grp") % 2)
    for j in range(far):
        for c in range(limit):
            at = (j * limit + c) * width
            out_ref[at : at + width] = coded(limit, rate_ref, where, me ^ (first + j), c)


def keep_body(n, limit, pair_ref, count_ref, rate_ref, got_ref, *rest):
    far, width = n // 2, rate_ref.shape[1]
    outs, where = rest[:far], rest[far]
    slots(n, limit, pair_ref, count_ref, where)
    me = lax.axis_index("row")
    first = far * (lax.axis_index("grp") % 2)
    rows = limit * width
    for j in range(far):
        for c in range(limit):
            outs[j][c * width : (c + 1) * width] = coded(
                limit, rate_ref, where, me ^ (first + j), c
            )
        outs[j][rows:] = got_ref[j * rows : (j + 1) * rows]


def gram_body(item_ref, gram_ref):
    items = item_ref[...]
    gram_ref[...] = lax.dot_general(items, items, COLS, preferred_element_type=F32).astype(BF)


def block_at(send_refs, t, c, peer, width):
    return pl.ds(pl.multiple_of(send_refs[t][c, peer] * width, width), width)


def peer_of(n, j):
    return lax.axis_index("row") ^ (n // 2 * (lax.axis_index("grp") % 2) + j)


def user_terms(n, limit, width, j, send_refs, item_ref, gram, user_ref, code_ref, keep):
    terms = []
    for t in range(2):
        left = user_ref[t * width : (t + 1) * width]
        total = jnp.dot(left, gram, preferred_element_type=F32)
        for c in range(limit):
            right = item_ref[block_at(send_refs, t, c, peer_of(n, j), width)]
            at = (t * limit + c) * width
            code = code_ref[at : at + width].astype(jnp.int32) + OFFSET
            weighted = CONFIDENCE * (code.astype(F32) * (1.0 / STEPS))
            score = lax.dot_general(left, right, ROWS, preferred_element_type=F32)
            error = jnp.where(code > 0, weighted * score - 1.0 - weighted, 0.0).astype(BF)
            total += jnp.dot(error, right, preferred_element_type=F32)
            keep(t, c, error)
        terms.append(total)
    return terms


def add_items(n, limit, width, j, send_refs, user_ref, t, c, error, sum_ref):
    left = user_ref[t * width : (t + 1) * width]
    term = lax.dot_general(error, left, COLS, preferred_element_type=F32)
    sum_ref[block_at(send_refs, t, c, peer_of(n, j), width)] += term.astype(BF).astype(F32)


def first_body(n, limit, width, own_ref, oth_ref, item_ref, gram_ref, user_ref, code_ref, *outs):
    out_ref, sum_ref, cross_ref = outs
    sends = (own_ref, oth_ref)
    sum_ref[...] = jnp.zeros_like(sum_ref)

    def keep(t, c, error):
        add_items(n, limit, width, 0, sends, user_ref, t, c, error, sum_ref)

    terms = user_terms(
        n, limit, width, 0, sends, item_ref, gram_ref[...], user_ref, code_ref, keep
    )
    for t in range(2):
        out_ref[t * width : (t + 1) * width] = terms[t]
    users = user_ref[...]
    cross_ref[...] = lax.dot_general(users, users, COLS, preferred_element_type=F32)


def users_body(n, limit, width, own_ref, oth_ref, item_ref, gram_ref, *rest):
    m = n // 2 - 1
    users, codes, outs, error_ref = rest[:m], rest[m : 2 * m], rest[2 * m : 3 * m], rest[3 * m]
    gram = gram_ref[...]
    for j in range(m):
        def keep(t, c, error):
            error_ref[(j * 2 + t) * limit + c] = error

        terms = user_terms(
            n, limit, width, j + 1, (own_ref, oth_ref), item_ref, gram, users[j], codes[j], keep
        )
        for t in range(2):
            outs[j][t * width : (t + 1) * width] = terms[t].astype(BF)


def items_body(n, limit, width, own_ref, oth_ref, item_ref, part_ref, cross_ref, error_ref, *rest):
    m = n // 2 - 1
    users, (mine_ref, other_ref, sum_ref) = rest[:m], rest[m:]
    cross = cross_ref[...]
    for j in range(m):
        block = users[j][...]
        cross += lax.dot_general(block, block, COLS, preferred_element_type=F32)
    sum_ref[...] = part_ref[...] + jnp.dot(
        item_ref[...], cross.astype(BF), preferred_element_type=F32
    )
    for j in range(m):
        for t in range(2):
            for c in range(limit):
                error = error_ref[(j * 2 + t) * limit + c]
                add_items(
                    n, limit, width, j + 1, (own_ref, oth_ref), users[j], t, c, error, sum_ref
                )
    core = lax.axis_index("grp") % 2
    half = mine_ref.shape[0]
    mine_ref[...] = sum_ref[pl.ds(pl.multiple_of(core * half, half), half)]
    other_ref[...] = sum_ref[pl.ds(pl.multiple_of((1 - core) * half, half), half)].astype(BF)


def swap(x, axis, k):
    return lax.ppermute(x, axis, [(i, i ^ k) for i in range(lax.axis_size(axis))])


def swap_by_core(x, j):
    n, grp_n = lax.axis_size("row"), lax.axis_size("grp")
    pairs = [(g * n + r, g * n + (r ^ (n // 2 * (g % 2) + j))) for g in range(grp_n) for r in range(n)]
    return lax.ppermute(x, ("grp", "row"), pairs)


def shards(users, items, ratings, pair_list, send_list, counts):
    n = lax.axis_size("row")
    grp_n = lax.axis_size("grp")
    width = ratings.shape[2]
    factors = users.shape[1]
    limit = send_list.shape[2]
    item_rows = items.shape[0]
    user_rows = users.shape[0]
    far = n // 2
    total_users = user_rows * grp_n * n
    total_items = item_rows * n
    sds = jax.ShapeDtypeStruct
    table = pltpu.SMEM((n * limit,), jnp.int32)

    pairs = jnp.swapaxes(pair_list[0], 0, 1)
    sends = jnp.swapaxes(send_list[0], 0, 1)
    sends = (sends, swap(sends, "grp", 1))

    both = jnp.concatenate([users, swap(users, "grp", 1)])
    blocks = [swap_by_core(both, 0)]
    blocks += [swap(blocks[0], "row", j) for j in range(1, far)]

    given = call(
        functools.partial(give_body, n, limit),
        sds((far * limit * width, width), jnp.int16),
        [SM, SM, VM],
        0,
        ratings.size * 3,
        [table],
    )(pairs, counts, ratings[0])
    codes = call(
        functools.partial(keep_body, n, limit),
        [sds((2 * limit * width, width), jnp.int16)] * far,
        [SM, SM, VM, VM],
        0,
        ratings.size * 3,
        [table],
    )(pairs, counts, ratings[0], swap(given, "grp", 1))
    codes = [swap_by_core(codes[j], j) for j in range(far)]

    pair_flops = 2 * 2 * limit * user_rows * factors * width
    cross_flops = 2 * 2 * user_rows * factors**2
    gram = call(
        gram_body, sds((factors, factors), BF), [VM], 2 * item_rows * factors**2, items.size * 2
    )(items)
    first, part, cross = call(
        functools.partial(first_body, n, limit, width),
        [
            sds((2 * user_rows, factors), F32),
            sds((item_rows, factors), F32),
            sds((factors, factors), F32),
        ],
        [SM, SM, VM, VM, VM, VM],
        3 * pair_flops + 2 * cross_flops,
        4 << 20,
    )(*sends, items, gram, blocks[0], codes[0])
    *terms, errors = call(
        functools.partial(users_body, n, limit, width),
        [sds((2 * user_rows, factors), BF)] * (far - 1)
        + [sds(((far - 1) * 2 * limit, user_rows, width), BF)],
        [SM, SM, VM, VM] + [VM] * (2 * far - 2),
        (far - 1) * (2 * pair_flops + cross_flops),
        4 << 20,
    )(*sends, items, gram, *blocks[1:], *codes[1:])
    half = item_rows // 2
    mine, other = call(
        functools.partial(items_body, n, limit, width),
        [sds((half, factors), F32), sds((half, factors), BF)],
        [SM, SM, VM, VM, VM, VM] + [VM] * (far - 1),
        (far - 1) * (pair_flops + cross_flops) + 2 * item_rows * factors**2,
        8 << 20,
        [pltpu.VMEM((item_rows, factors), F32)],
    )(*sends, items, part, cross, errors, *blocks[1:])

    user_sum = first
    for j in range(1, far):
        user_sum += swap(terms[j - 1], "row", j).astype(F32)
    user_sum = swap_by_core(user_sum.astype(BF), 0)
    user_sum = user_sum[:user_rows].astype(F32) + swap(user_sum[user_rows:], "grp", 1).astype(F32)
    new_users = users.astype(F32) - 4.0 / math.sqrt(total_items) * user_sum

    core = lax.axis_index("grp") % 2
    pair_sum = mine + swap(other, "grp", 1).astype(F32)
    if grp_n == 4:
        here = pair_sum.astype(BF)
        there = swap(here, "grp", 2)
        one = here.astype(F32) + there.astype(F32)
        two = swap(here, "grp", 1).astype(F32) + swap(there, "grp", 1).astype(F32)
    else:
        peers = [list(range(c, grp_n, 2)) for c in range(2)]
        one = lax.psum(pair_sum, "grp", axis_index_groups=peers)
        two = swap(one, "grp", 1)
    item_sum = jnp.where(core == 0, jnp.concatenate([one, two]), jnp.concatenate([two, one]))
    new_items = items.astype(F32) - 8.0 / math.sqrt(total_users) * item_sum
    return (new_users, new_items)


def solution(mesh):
    in_specs = (
        P(("grp", "row"), None),
        P("row", None),
        P(("grp", "row"), None, None, None),
        P(("grp", "row"), None, None),
        P(("grp", "row"), None, None),
        P(("grp", "row")),
    )
    out_specs = (P(("grp", "row"), None), P("row", None))
    return jax.shard_map(shards, mesh=mesh, in_specs=in_specs, out_specs=out_specs, check_vma=False)
```

```python
import functools
import math

import jax
import jax.numpy as jnp
from jax import lax
from jax.experimental import pallas as pl
from jax.experimental.pallas import tpu as pltpu
from jax.sharding import PartitionSpec as P

CONFIDENCE = 40.0
STEPS = 65535.0
OFFSET = 32768
BF = jnp.bfloat16
F32 = jnp.float32

VM = pl.BlockSpec(memory_space=pltpu.VMEM)
SM = pl.BlockSpec(memory_space=pltpu.SMEM)
ANY = pl.BlockSpec(memory_space=pl.ANY)
ROWS = (((1,), (1,)), ((), ()))
COLS = (((0,), (0,)), ((), ()))


def call(body, outs, in_specs, flops, moved, scratch=(), mib=24):
    return pl.pallas_call(
        body,
        out_shape=outs,
        in_specs=in_specs,
        out_specs=jax.tree.map(lambda _: VM, outs),
        scratch_shapes=scratch,
        compiler_params=pltpu.CompilerParams(vmem_limit_bytes=mib << 20),
        cost_estimate=pl.CostEstimate(flops=flops, bytes_accessed=moved, transcendentals=0),
    )


def spread_body(n, limit, pair_ref, count_ref, rate_ref, *rest):
    outs, where = rest[: n // 2], rest[n // 2]
    me, (blocks, width, _) = lax.axis_index("row"), rate_ref.shape
    for s in range(n * limit):
        where[s] = -1
    for i in range(blocks):
        @pl.when(i < count_ref[0])
        def _():
            where[pair_ref[1, i]] = i
    for j, out_ref in enumerate(outs):
        for side in range(2):
            for c in range(limit):
                i = where[(me ^ (2 * j + side)) * limit + c]
                rate = rate_ref[jnp.maximum(i, 0)]
                code = jnp.where(i >= 0, (rate * STEPS + 0.5).astype(jnp.int32), 0) - OFFSET
                at = (side * limit + c) * width
                out_ref[at : at + width] = code.astype(jnp.int16)


def halves_body(*refs):
    out_ref = refs[-1]
    for j, ref in enumerate(refs[:-1]):
        rows = ref.shape[0] // 2
        out_ref[j * rows : (j + 1) * rows] = ref[rows:]


def gram_body(item_ref, gram_ref, copy_ref, sem):
    copy = pltpu.make_async_copy(item_ref, copy_ref, sem)
    copy.start()
    copy.wait()
    items = copy_ref[...]
    gram_ref[...] = lax.dot_general(items, items, COLS, preferred_element_type=F32).astype(BF)


def score_body(m, more, item_ref, gram_ref, *rest):
    users, rest = rest[:m], rest[m:]
    total, rest = (rest[0][...], rest[1:]) if more else (None, rest)
    score_ref, user_ref, last_ref, all_ref = rest
    width = users[0].shape[0]
    for j in range(m):
        all_ref[j * width : (j + 1) * width] = users[j][...]
    every = all_ref[...]
    score_ref[...] = lax.dot_general(every, item_ref[...], ROWS, preferred_element_type=F32)
    user_ref[...] = jnp.dot(every, gram_ref[...], preferred_element_type=F32)
    cross = lax.dot_general(every, every, COLS, preferred_element_type=F32)
    if more:
        cross = (total + cross).astype(BF)
        last_ref[...] = jnp.dot(item_ref[...], cross, preferred_element_type=F32)
    else:
        last_ref[...] = cross


def error_body(n, limit, width, send_ref, item_ref, near_ref, far_ref, near_gram, far_gram, part_ref, *rest):
    far = n // 2
    users, codes, outs = rest[:n], rest[n : n + far + 1], rest[n + far + 1 : 2 * n + far + 1]
    mine_ref, other_ref, sum_ref = rest[2 * n + far + 1 :]
    me = lax.axis_index("row")
    core = lax.axis_index("grp") % 2
    sum_ref[...] = part_ref[...]
    for k in [*range(far, n), *range(far)]:
        left = users[k][...]
        score_ref, gram_ref, row = (near_ref, near_gram, k) if k < far else (far_ref, far_gram, k - far)
        row = slice(row * width, (row + 1) * width)
        errors, rights, spots = [], [], []
        for c in range(limit):
            at = pl.ds(pl.multiple_of(send_ref[c, me ^ k] * width, width), width)
            code_ref, place = (codes[k // 2], c) if k % 2 == 0 else (codes[far], k // 2 * limit + c)
            code = code_ref[place * width : (place + 1) * width].astype(jnp.int32) + OFFSET
            weighted = CONFIDENCE * (code.astype(F32) * (1.0 / STEPS))
            error = weighted * score_ref[row, at] - 1.0 - weighted
            errors.append(jnp.where(code > 0, error, 0.0).astype(BF))
            rights.append(item_ref[at])
            spots.append(at)
        error = jnp.concatenate(errors, axis=1)
        total = gram_ref[row] + jnp.dot(
            error, jnp.concatenate(rights), preferred_element_type=F32
        )
        outs[k][...] = total.astype(outs[k].dtype)
        terms = lax.dot_general(error, left, COLS, preferred_element_type=F32)
        for c, at in enumerate(spots):
            sum_ref[at] += terms[c * width : (c + 1) * width].astype(BF).astype(F32)
    half = mine_ref.shape[0]
    other_ref[...] = sum_ref[pl.ds(pl.multiple_of((1 - core) * half, half), half)].astype(BF)
    mine_ref[...] = sum_ref[pl.ds(pl.multiple_of(core * half, half), half)]


def swap(x, axis, k):
    return lax.ppermute(x, axis, [(i, i ^ k) for i in range(lax.axis_size(axis))])


def shards(users, items, ratings, pair_list, send_list, counts):
    n = lax.axis_size("row")
    grp_n = lax.axis_size("grp")
    width = ratings.shape[2]
    factors = users.shape[1]
    limit = send_list.shape[2]
    item_rows = items.shape[0]
    user_rows = users.shape[0]
    far = n // 2
    total_users = user_rows * grp_n * n
    total_items = item_rows * n
    sds = jax.ShapeDtypeStruct

    pairs = jnp.swapaxes(pair_list[0], 0, 1)
    sends = jnp.swapaxes(send_list[0], 0, 1)

    over = swap(users, "row", far)
    codes = call(
        functools.partial(spread_body, n, limit),
        [sds((2 * limit * width, width), jnp.int16)] * far,
        [SM, SM, VM],
        0,
        ratings.size * 6,
        [pltpu.SMEM((n * limit,), jnp.int32)],
    )(pairs, counts, ratings[0])
    blocks = [users] + [swap(users, "row", k) for k in range(1, far)]
    blocks[1], *late = lax.optimization_barrier((blocks[1], *codes[1 : far // 2]))
    blocks += [over] + [swap(over, "row", k) for k in range(1, far)]
    along = {j: swap(codes[j], "row", 2 * j) for j in range(far // 2, far)}
    along.update({j: swap(late[j - 1], "row", 2 * j) for j in range(1, far // 2)})
    along = [codes[0]] + [along[j] for j in range(1, far)]
    passed = call(
        halves_body,
        sds((far * limit * width, width), jnp.int16),
        [VM] * far,
        2 * 10**10,
        4 * far * limit * width * width,
    )(*along)
    codes = [*along, swap(passed, "row", 1)]

    cross_flops = 2 * user_rows * factors**2
    item_flops = 2 * item_rows * factors**2
    score_flops = 2 * user_rows * factors * item_rows
    gram, rows = call(
        gram_body,
        [sds((factors, factors), BF), sds((item_rows, factors), BF)],
        [ANY],
        item_flops,
        items.size * 4,
        [pltpu.SemaphoreType.DMA],
    )(items)
    score_out = [sds((far * user_rows, item_rows), F32), sds((far * user_rows, factors), F32)]
    every = [pltpu.VMEM((far * user_rows, factors), BF)]
    near_score, near_gram, cross = call(
        functools.partial(score_body, far, False),
        score_out + [sds((factors, factors), F32)],
        [VM] * (2 + far),
        40 * far * (score_flops + 2 * cross_flops),
        4 << 20,
        every,
    )(rows, gram, *blocks[:far])
    far_score, far_gram, item_part = call(
        functools.partial(score_body, far, True),
        score_out + [sds((item_rows, factors), F32)],
        [VM] * (3 + far),
        40 * (far * (score_flops + 2 * cross_flops) + item_flops),
        4 << 20,
        every,
    )(rows, gram, *blocks[far:], cross)
    half = item_rows // 2
    *parts, mine, other = call(
        functools.partial(error_body, n, limit, width),
        [sds((user_rows, factors), F32 if k in (0, far) else BF) for k in range(n)]
        + [sds((half, factors), F32), sds((half, factors), BF)],
        [SM] + [VM] * (7 + n + far),
        8 * n * limit * user_rows * factors * width,
        8 << 20,
        [pltpu.VMEM((item_rows, factors), F32)],
    )(sends, rows, near_score, far_score, near_gram, far_gram, item_part, *blocks, *codes)

    across = parts[far]
    for k in range(1, far):
        across += swap(parts[far + k], "row", k).astype(F32)
    user_sum = parts[0]
    for k in range(1, far):
        user_sum += swap(parts[k], "row", k).astype(F32)
    user_sum += swap(across.astype(BF), "row", far).astype(F32)
    new_users = users.astype(F32) - 4.0 / math.sqrt(total_items) * user_sum

    core = lax.axis_index("grp") % 2
    pair_sum = mine + swap(other, "grp", 1).astype(F32)
    if grp_n == 4:
        here = pair_sum.astype(BF)
        there = swap(here, "grp", 2)
        first = here.astype(F32) + there.astype(F32)
        second = swap(here, "grp", 1).astype(F32) + swap(there, "grp", 1).astype(F32)
    else:
        peers = [list(range(c, grp_n, 2)) for c in range(2)]
        first = lax.psum(pair_sum, "grp", axis_index_groups=peers)
        second = swap(first, "grp", 1)
    item_sum = jnp.where(
        core == 0, jnp.concatenate([first, second]), jnp.concatenate([second, first])
    )
    new_items = rows.astype(F32) - 8.0 / math.sqrt(total_users) * item_sum
    return (new_users, new_items)


def solution(mesh):
    in_specs = (
        P(("grp", "row"), None),
        P("row", None),
        P(("grp", "row"), None, None, None),
        P(("grp", "row"), None, None),
        P(("grp", "row"), None, None),
        P(("grp", "row")),
    )
    out_specs = (P(("grp", "row"), None), P("row", None))
    return jax.shard_map(shards, mesh=mesh, in_specs=in_specs, out_specs=out_specs, check_vma=False)
```

```python
import functools
import math

import jax
import jax.numpy as jnp
from jax import lax
from jax.experimental import pallas as pl
from jax.experimental.pallas import tpu as pltpu
from jax.sharding import PartitionSpec as P

CONFIDENCE = 40.0
STEPS = 65535.0
OFFSET = 32768
BF = jnp.bfloat16
F32 = jnp.float32

VM = pl.BlockSpec(memory_space=pltpu.VMEM)
SM = pl.BlockSpec(memory_space=pltpu.SMEM)
ANY = pl.BlockSpec(memory_space=pl.ANY)
ROWS = (((1,), (1,)), ((), ()))
COLS = (((0,), (0,)), ((), ()))


def call(body, outs, in_specs, flops, moved, scratch=(), mib=24):
    return pl.pallas_call(
        body,
        out_shape=outs,
        in_specs=in_specs,
        out_specs=jax.tree.map(lambda _: VM, outs),
        scratch_shapes=scratch,
        compiler_params=pltpu.CompilerParams(vmem_limit_bytes=mib << 20),
        cost_estimate=pl.CostEstimate(flops=flops, bytes_accessed=moved, transcendentals=0),
    )


def spread_body(n, limit, pair_ref, count_ref, rate_ref, *rest):
    outs, where = rest[: n // 2], rest[n // 2]
    me, (blocks, width, _) = lax.axis_index("row"), rate_ref.shape
    for s in range(n * limit):
        where[s] = -1
    for i in range(blocks):
        @pl.when(i < count_ref[0])
        def _():
            where[pair_ref[1, i]] = i
    for j, out_ref in enumerate(outs):
        for side in range(2):
            for c in range(limit):
                i = where[(me ^ (2 * j + side)) * limit + c]
                rate = rate_ref[jnp.maximum(i, 0)]
                code = jnp.where(i >= 0, (rate * STEPS + 0.5).astype(jnp.int32), 0) - OFFSET
                at = (side * limit + c) * width
                out_ref[at : at + width] = code.astype(jnp.int16)


def halves_body(*refs):
    out_ref = refs[-1]
    for j, ref in enumerate(refs[:-1]):
        rows = ref.shape[0] // 2
        out_ref[j * rows : (j + 1) * rows] = ref[rows:]


def gram_body(item_ref, gram_ref, copy_ref, sem):
    copy = pltpu.make_async_copy(item_ref, copy_ref, sem)
    copy.start()
    copy.wait()
    items = copy_ref[...]
    gram_ref[...] = lax.dot_general(items, items, COLS, preferred_element_type=F32).astype(BF)


def score_body(m, more, item_ref, gram_ref, *rest):
    users, rest = rest[:m], rest[m:]
    total, rest = (rest[0][...], rest[1:]) if more else (None, rest)
    score_ref, user_ref, last_ref, all_ref = rest
    width = users[0].shape[0]
    for j in range(m):
        all_ref[j * width : (j + 1) * width] = users[j][...]
    every = all_ref[...]
    score_ref[...] = lax.dot_general(every, item_ref[...], ROWS, preferred_element_type=F32)
    user_ref[...] = jnp.dot(every, gram_ref[...], preferred_element_type=F32)
    cross = lax.dot_general(every, every, COLS, preferred_element_type=F32)
    if more:
        cross = (total + cross).astype(BF)
        last_ref[...] = jnp.dot(item_ref[...], cross, preferred_element_type=F32)
    else:
        last_ref[...] = cross


def error_body(ks, far, limit, width, send_ref, item_ref, score_refs, gram_refs, users, codes, outs, sum_ref):
    me = lax.axis_index("row")
    for k, user_ref, out_ref in zip(ks, users, outs):
        left = user_ref[...]
        row = k % far
        row = slice(row * width, (row + 1) * width)
        errors, rights, spots = [], [], []
        for c in range(limit):
            at = pl.ds(pl.multiple_of(send_ref[c, me ^ k] * width, width), width)
            code_ref, place = (codes[k], c) if k % 2 == 0 else (codes[1], k // 2 * limit + c)
            code = code_ref[place * width : (place + 1) * width].astype(jnp.int32) + OFFSET
            weighted = CONFIDENCE * (code.astype(F32) * (1.0 / STEPS))
            error = weighted * score_refs[k // far][row, at] - 1.0 - weighted
            errors.append(jnp.where(code > 0, error, 0.0).astype(BF))
            rights.append(item_ref[at])
            spots.append(at)
        error = jnp.concatenate(errors, axis=1)
        total = gram_refs[k // far][row] + jnp.dot(
            error, jnp.concatenate(rights), preferred_element_type=F32
        )
        out_ref[...] = total.astype(out_ref.dtype)
        terms = lax.dot_general(error, left, COLS, preferred_element_type=F32)
        for c, at in enumerate(spots):
            sum_ref[at] += terms[c * width : (c + 1) * width].astype(BF).astype(F32)


def even_body(ks, far, limit, width, send_ref, item_ref, *rest):
    m = len(ks)
    score_refs, gram_refs, part_ref, rest = rest[:2], rest[2:4], rest[4], rest[5:]
    users, codes, outs, sum_ref = rest[:m], rest[m : 2 * m], rest[2 * m : 3 * m], rest[3 * m]
    sum_ref[...] = part_ref[...]
    error_body(
        ks, far, limit, width, send_ref, item_ref, score_refs, gram_refs, users,
        dict(zip(ks, codes)), outs, sum_ref,
    )


def odd_body(ks, far, limit, width, send_ref, item_ref, *rest):
    m = len(ks)
    score_refs, gram_refs, part_ref, rest = rest[:2], rest[2:4], rest[4], rest[5:]
    users, code_ref, rest = rest[:m], rest[m], rest[m + 1 :]
    outs, (mine_ref, other_ref, sum_ref) = rest[:m], rest[m:]
    sum_ref[...] = part_ref[...]
    error_body(
        ks, far, limit, width, send_ref, item_ref, score_refs, gram_refs, users,
        {1: code_ref}, outs, sum_ref,
    )
    core = lax.axis_index("grp") % 2
    half = mine_ref.shape[0]
    other_ref[...] = sum_ref[pl.ds(pl.multiple_of((1 - core) * half, half), half)].astype(BF)
    mine_ref[...] = sum_ref[pl.ds(pl.multiple_of(core * half, half), half)]


def swap(x, axis, k):
    return lax.ppermute(x, axis, [(i, i ^ k) for i in range(lax.axis_size(axis))])


def shards(users, items, ratings, pair_list, send_list, counts):
    n = lax.axis_size("row")
    grp_n = lax.axis_size("grp")
    width = ratings.shape[2]
    factors = users.shape[1]
    limit = send_list.shape[2]
    item_rows = items.shape[0]
    user_rows = users.shape[0]
    far = n // 2
    hop = n - 2 if n > 2 else 1
    total_users = user_rows * grp_n * n
    total_items = item_rows * n
    sds = jax.ShapeDtypeStruct

    pairs = jnp.swapaxes(pair_list[0], 0, 1)
    sends = jnp.swapaxes(send_list[0], 0, 1)

    over = swap(users, "row", far)
    codes = call(
        functools.partial(spread_body, n, limit),
        [sds((2 * limit * width, width), jnp.int16)] * far,
        [SM, SM, VM],
        0,
        ratings.size * 6,
        [pltpu.SMEM((n * limit,), jnp.int32)],
    )(pairs, counts, ratings[0])
    blocks = [users] + [swap(users, "row", k) for k in range(1, far)]
    blocks[1], *late = lax.optimization_barrier((blocks[1], *codes[1 : far // 2]))
    blocks += [over] + [swap(over, "row", k) for k in range(1, far)]
    along = {j: swap(codes[j], "row", 2 * j) for j in range(far // 2, far)}
    along.update({j: swap(late[j - 1], "row", 2 * j) for j in range(1, far // 2)})
    along = [codes[0]] + [along[j] for j in range(1, far)]
    passed = call(
        halves_body,
        sds((far * limit * width, width), jnp.int16),
        [VM] * far,
        2 * 10**10,
        4 * far * limit * width * width,
    )(*along)

    cross_flops = 2 * user_rows * factors**2
    item_flops = 2 * item_rows * factors**2
    score_flops = 2 * user_rows * factors * item_rows
    gram, rows = call(
        gram_body,
        [sds((factors, factors), BF), sds((item_rows, factors), BF)],
        [ANY],
        item_flops,
        items.size * 4,
        [pltpu.SemaphoreType.DMA],
    )(items)
    score_out = [sds((far * user_rows, item_rows), F32), sds((far * user_rows, factors), F32)]
    every = [pltpu.VMEM((far * user_rows, factors), BF)]
    near_score, near_gram, cross = call(
        functools.partial(score_body, far, False),
        score_out + [sds((factors, factors), F32)],
        [VM] * (2 + far),
        40 * far * (score_flops + 2 * cross_flops),
        4 << 20,
        every,
    )(rows, gram, *blocks[:far])
    far_score, far_gram, item_part = call(
        functools.partial(score_body, far, True),
        score_out + [sds((item_rows, factors), F32)],
        [VM] * (3 + far),
        40 * (far * (score_flops + 2 * cross_flops) + item_flops),
        4 << 20,
        every,
    )(rows, gram, *blocks[far:], cross)
    half = item_rows // 2
    pair_flops = 6 * limit * user_rows * factors * width
    passed = swap(passed, "row", 1)
    scores = (near_score, far_score, near_gram, far_gram)
    evens, odds = range(0, n, 2), [*range(far + 1, n, 2), *range(1, far, 2)]
    *even_terms, sums = call(
        functools.partial(even_body, evens, far, limit, width),
        [sds((user_rows, factors), F32 if k in (0, hop) else BF) for k in evens]
        + [sds((item_rows, factors), F32)],
        [SM] + [VM] * (6 + 2 * len(evens)),
        1 * len(evens) * pair_flops,
        4 << 20,
    )(sends, rows, *scores, item_part, *[blocks[k] for k in evens], *along)
    *odd_terms, mine, other = call(
        functools.partial(odd_body, odds, far, limit, width),
        [sds((user_rows, factors), BF)] * len(odds)
        + [sds((half, factors), F32), sds((half, factors), BF)],
        [SM] + [VM] * (7 + len(odds)),
        0 * len(odds) * pair_flops,
        0,
        [pltpu.VMEM((item_rows, factors), F32)],
    )(sends, rows, *scores, sums, *[blocks[k] for k in odds], passed)
    parts = dict(zip([*evens, *odds], [*even_terms, *odd_terms]))

    across = parts[hop]
    for k in range(1, far):
        across += swap(parts[hop ^ k], "row", k).astype(F32)
    user_sum = parts[0]
    for k in range(1, far):
        user_sum += swap(parts[k], "row", k).astype(F32)
    user_sum += swap(across.astype(BF), "row", hop).astype(F32)
    new_users = users.astype(F32) - 4.0 / math.sqrt(total_items) * user_sum

    core = lax.axis_index("grp") % 2
    pair_sum = mine + swap(other, "grp", 1).astype(F32)
    if grp_n == 4:
        here = pair_sum.astype(BF)
        there = swap(here, "grp", 2)
        first = here.astype(F32) + there.astype(F32)
        second = swap(here, "grp", 1).astype(F32) + swap(there, "grp", 1).astype(F32)
    else:
        peers = [list(range(c, grp_n, 2)) for c in range(2)]
        first = lax.psum(pair_sum, "grp", axis_index_groups=peers)
        second = swap(first, "grp", 1)
    item_sum = jnp.where(
        core == 0, jnp.concatenate([first, second]), jnp.concatenate([second, first])
    )
    new_items = rows.astype(F32) - 8.0 / math.sqrt(total_users) * item_sum
    return (new_users, new_items)


def solution(mesh):
    in_specs = (
        P(("grp", "row"), None),
        P("row", None),
        P(("grp", "row"), None, None, None),
        P(("grp", "row"), None, None),
        P(("grp", "row"), None, None),
        P(("grp", "row")),
    )
    out_specs = (P(("grp", "row"), None), P("row", None))
    return jax.shard_map(shards, mesh=mesh, in_specs=in_specs, out_specs=out_specs, check_vma=False)
```

```python
import functools
import math

import jax
import jax.numpy as jnp
from jax import lax
from jax.experimental import pallas as pl
from jax.experimental.pallas import tpu as pltpu
from jax.sharding import PartitionSpec as P

CONFIDENCE = 40.0
STEPS = 65535.0
OFFSET = 32768
PARTS = 3
BF = jnp.bfloat16
F32 = jnp.float32

VM = pl.BlockSpec(memory_space=pltpu.VMEM)
SM = pl.BlockSpec(memory_space=pltpu.SMEM)
ANY = pl.BlockSpec(memory_space=pl.ANY)
ROWS = (((1,), (1,)), ((), ()))
COLS = (((0,), (0,)), ((), ()))


def call(body, outs, in_specs, flops, moved, scratch=(), mib=24):
    return pl.pallas_call(
        body,
        out_shape=outs,
        in_specs=in_specs,
        out_specs=jax.tree.map(lambda _: VM, outs),
        scratch_shapes=scratch,
        compiler_params=pltpu.CompilerParams(vmem_limit_bytes=mib << 20),
        cost_estimate=pl.CostEstimate(flops=flops, bytes_accessed=moved, transcendentals=0),
    )


def spread_body(n, limit, pair_ref, count_ref, rate_ref, *rest):
    outs, where = rest[: n // 2], rest[n // 2]
    me, (blocks, width, _) = lax.axis_index("row"), rate_ref.shape
    for s in range(n * limit):
        where[s] = -1
    for i in range(blocks):
        @pl.when(i < count_ref[0])
        def _():
            where[pair_ref[1, i]] = i
    for j, out_ref in enumerate(outs):
        for side in range(2):
            for c in range(limit):
                i = where[(me ^ (2 * j + side)) * limit + c]
                rate = rate_ref[jnp.maximum(i, 0)]
                code = jnp.where(i >= 0, (rate * STEPS + 0.5).astype(jnp.int32), 0) - OFFSET
                at = (side * limit + c) * width
                out_ref[at : at + width] = code.astype(jnp.int16)


def halves_body(*refs):
    out_ref = refs[-1]
    for j, ref in enumerate(refs[:-1]):
        rows = ref.shape[0] // 2
        out_ref[j * rows : (j + 1) * rows] = ref[rows:]


def gram_body(item_ref, gram_ref, copy_ref, sem):
    copy = pltpu.make_async_copy(item_ref, copy_ref, sem)
    copy.start()
    copy.wait()
    items = copy_ref[...]
    gram_ref[...] = lax.dot_general(items, items, COLS, preferred_element_type=F32).astype(BF)


def score_body(m, more, item_ref, gram_ref, *rest):
    users, rest = rest[:m], rest[m:]
    total, rest = (rest[0][...], rest[1:]) if more else (None, rest)
    score_ref, user_ref, last_ref, all_ref = rest
    width = users[0].shape[0]
    for j in range(m):
        all_ref[j * width : (j + 1) * width] = users[j][...]
    every = all_ref[...]
    score_ref[...] = lax.dot_general(every, item_ref[...], ROWS, preferred_element_type=F32)
    user_ref[...] = jnp.dot(every, gram_ref[...], preferred_element_type=F32)
    cross = lax.dot_general(every, every, COLS, preferred_element_type=F32)
    if more:
        cross = (total + cross).astype(BF)
        last_ref[...] = jnp.dot(item_ref[...], cross, preferred_element_type=F32)
    else:
        last_ref[...] = cross


def error_body(ks, far, limit, width, send_ref, item_ref, score_refs, gram_refs, users, codes, outs, sum_ref):
    me = lax.axis_index("row")
    for k, user_ref, out_ref in zip(ks, users, outs):
        left = user_ref[...]
        row = k % far
        row = slice(row * width, (row + 1) * width)
        errors, rights, spots = [], [], []
        for c in range(limit):
            at = pl.ds(pl.multiple_of(send_ref[c, me ^ k] * width, width), width)
            code_ref, place = (codes[k], c) if k % 2 == 0 else (codes[1], k // 2 * limit + c)
            code = code_ref[place * width : (place + 1) * width].astype(jnp.int32) + OFFSET
            weighted = CONFIDENCE * (code.astype(F32) * (1.0 / STEPS))
            error = weighted * score_refs[k // far][row, at] - 1.0 - weighted
            errors.append(jnp.where(code > 0, error, 0.0).astype(BF))
            rights.append(item_ref[at])
            spots.append(at)
        error = jnp.concatenate(errors, axis=1)
        total = gram_refs[k // far][row] + jnp.dot(
            error, jnp.concatenate(rights), preferred_element_type=F32
        )
        out_ref[...] = total.astype(out_ref.dtype)
        terms = lax.dot_general(error, left, COLS, preferred_element_type=F32)
        for c, at in enumerate(spots):
            sum_ref[at] += terms[c * width : (c + 1) * width].astype(BF).astype(F32)


def even_body(ks, far, limit, width, send_ref, item_ref, *rest):
    m = len(ks)
    score_refs, gram_refs, part_ref, rest = rest[:2], rest[2:4], rest[4], rest[5:]
    users, codes, outs, sum_ref = rest[:m], rest[m : 2 * m], rest[2 * m : 3 * m], rest[3 * m]
    sum_ref[...] = part_ref[...]
    error_body(
        ks, far, limit, width, send_ref, item_ref, score_refs, gram_refs, users,
        dict(zip(ks, codes)), outs, sum_ref,
    )


def odd_body(ks, far, limit, width, send_ref, item_ref, *rest):
    m = len(ks)
    score_refs, gram_refs, part_ref, rest = rest[:2], rest[2:4], rest[4], rest[5:]
    users, code_ref, rest = rest[:m], rest[m], rest[m + 1 :]
    outs, (mine_ref, other_ref, sum_ref) = rest[:m], rest[m:]
    sum_ref[...] = part_ref[...]
    error_body(
        ks, far, limit, width, send_ref, item_ref, score_refs, gram_refs, users,
        {1: code_ref}, outs, sum_ref,
    )
    core = lax.axis_index("grp") % 2
    half = mine_ref.shape[0]
    other_ref[...] = sum_ref[pl.ds(pl.multiple_of((1 - core) * half, half), half)].astype(BF)
    mine_ref[...] = sum_ref[pl.ds(pl.multiple_of(core * half, half), half)]


def total_body(*refs):
    total = refs[0][...]
    for ref in refs[1:-1]:
        total += ref[...].astype(F32)
    refs[-1][...] = total


def finish_body(user_scale, item_scale, user_ref, total_ref, item_ref, *rest):
    pieces, (users_out, items_out, buf, sems) = rest[:-4], rest[-4:]
    core = lax.axis_index("grp") % 2
    half = pieces[0].shape[0]
    step = half // PARTS
    copies = []
    for side in range(2):
        first = (core + side) % 2 * half
        mine = pieces[side * (len(pieces) // 2) : (side + 1) * (len(pieces) // 2)]
        for i in range(PARTS):
            part = slice(i * step, (i + 1) * step)
            at = pl.ds(pl.multiple_of(first + i * step, step), step)
            total = mine[0][part].astype(F32)
            for piece in mine[1:]:
                total += piece[part].astype(F32)
            buf[at] = item_ref[at].astype(F32) - item_scale * total
            copies.append(
                pltpu.make_async_copy(buf.at[at], items_out.at[at], sems.at[side * PARTS + i])
            )
            copies[-1].start()
    users_out[...] = user_ref[...].astype(F32) - user_scale * total_ref[...]
    for copy in copies:
        copy.wait()


def swap(x, axis, k):
    return lax.ppermute(x, axis, [(i, i ^ k) for i in range(lax.axis_size(axis))])


def shards(users, items, ratings, pair_list, send_list, counts):
    n = lax.axis_size("row")
    grp_n = lax.axis_size("grp")
    width = ratings.shape[2]
    factors = users.shape[1]
    limit = send_list.shape[2]
    item_rows = items.shape[0]
    user_rows = users.shape[0]
    far = n // 2
    hop = n - 2 if n > 2 else 1
    total_users = user_rows * grp_n * n
    total_items = item_rows * n
    sds = jax.ShapeDtypeStruct

    pairs = jnp.swapaxes(pair_list[0], 0, 1)
    sends = jnp.swapaxes(send_list[0], 0, 1)

    over = swap(users, "row", far)
    codes = call(
        functools.partial(spread_body, n, limit),
        [sds((2 * limit * width, width), jnp.int16)] * far,
        [SM, SM, VM],
        0,
        ratings.size * 6,
        [pltpu.SMEM((n * limit,), jnp.int32)],
    )(pairs, counts, ratings[0])
    blocks = [users] + [swap(users, "row", k) for k in range(1, far)]
    blocks[1], *late = lax.optimization_barrier((blocks[1], *codes[1 : far // 2]))
    blocks += [over] + [swap(over, "row", k) for k in range(1, far)]
    along = {j: swap(codes[j], "row", 2 * j) for j in range(far // 2, far)}
    along.update({j: swap(late[j - 1], "row", 2 * j) for j in range(1, far // 2)})
    along = [codes[0]] + [along[j] for j in range(1, far)]
    passed = call(
        halves_body,
        sds((far * limit * width, width), jnp.int16),
        [VM] * far,
        2 * 10**10,
        4 * far * limit * width * width,
    )(*along)

    cross_flops = 2 * user_rows * factors**2
    item_flops = 2 * item_rows * factors**2
    score_flops = 2 * user_rows * factors * item_rows
    gram, rows = call(
        gram_body,
        [sds((factors, factors), BF), sds((item_rows, factors), BF)],
        [ANY],
        item_flops,
        items.size * 4,
        [pltpu.SemaphoreType.DMA],
    )(items)
    score_out = [sds((far * user_rows, item_rows), F32), sds((far * user_rows, factors), F32)]
    every = [pltpu.VMEM((far * user_rows, factors), BF)]
    near_score, near_gram, cross = call(
        functools.partial(score_body, far, False),
        score_out + [sds((factors, factors), F32)],
        [VM] * (2 + far),
        40 * far * (score_flops + 2 * cross_flops),
        4 << 20,
        every,
    )(rows, gram, *blocks[:far])
    far_score, far_gram, item_part = call(
        functools.partial(score_body, far, True),
        score_out + [sds((item_rows, factors), F32)],
        [VM] * (3 + far),
        40 * (far * (score_flops + 2 * cross_flops) + item_flops),
        4 << 20,
        every,
    )(rows, gram, *blocks[far:], cross)
    half = item_rows // 2
    pair_flops = 6 * limit * user_rows * factors * width
    passed = swap(passed, "row", 1)
    scores = (near_score, far_score, near_gram, far_gram)
    evens, odds = range(0, n, 2), [*range(far + 1, n, 2), *range(1, far, 2)]
    *even_terms, sums = call(
        functools.partial(even_body, evens, far, limit, width),
        [sds((user_rows, factors), F32 if k in (0, hop) else BF) for k in evens]
        + [sds((item_rows, factors), F32)],
        [SM] + [VM] * (6 + 2 * len(evens)),
        1 * len(evens) * pair_flops,
        4 << 20,
    )(sends, rows, *scores, item_part, *[blocks[k] for k in evens], *along)
    *odd_terms, mine, other = call(
        functools.partial(odd_body, odds, far, limit, width),
        [sds((user_rows, factors), BF)] * len(odds)
        + [sds((half, factors), F32), sds((half, factors), BF)],
        [SM] + [VM] * (7 + len(odds)),
        0 * len(odds) * pair_flops,
        0,
        [pltpu.VMEM((item_rows, factors), F32)],
    )(sends, rows, *scores, sums, *[blocks[k] for k in odds], passed)
    parts = dict(zip([*evens, *odds], [*even_terms, *odd_terms]))

    across = parts[hop]
    for k in range(1, far):
        across += swap(parts[hop ^ k], "row", k).astype(F32)
    terms = [parts[0], swap(across.astype(BF), "row", hop)]
    terms += [swap(parts[k], "row", k) for k in range(1, far)]
    user_sum = call(
        total_body, sds((user_rows, factors), F32), [VM] * len(terms), 5 * 10**9, 16 * user_rows * factors
    )(*terms)

    pair_sum = mine + swap(other, "grp", 1).astype(F32)
    if grp_n == 4:
        here = pair_sum.astype(BF)
        there = swap(here, "grp", 2)
        pieces = [here, there, swap(here, "grp", 1), swap(there, "grp", 1)]
    else:
        peers = [list(range(c, grp_n, 2)) for c in range(2)]
        here = lax.psum(pair_sum, "grp", axis_index_groups=peers)
        pieces = [here, swap(here, "grp", 1)]
    new_users, new_items = pl.pallas_call(
        functools.partial(
            finish_body, 4.0 / math.sqrt(total_items), 8.0 / math.sqrt(total_users)
        ),
        out_shape=[sds((user_rows, factors), F32), sds((item_rows, factors), F32)],
        in_specs=[VM] * (3 + len(pieces)),
        out_specs=[VM, ANY],
        scratch_shapes=[
            pltpu.VMEM((item_rows, factors), F32),
            pltpu.SemaphoreType.DMA((2 * PARTS,)),
        ],
        compiler_params=pltpu.CompilerParams(vmem_limit_bytes=24 << 20),
        cost_estimate=pl.CostEstimate(flops=0, bytes_accessed=4 << 20, transcendentals=0),
    )(users, user_sum, rows, *pieces)
    return (new_users, new_items)


def solution(mesh):
    in_specs = (
        P(("grp", "row"), None),
        P("row", None),
        P(("grp", "row"), None, None, None),
        P(("grp", "row"), None, None),
        P(("grp", "row"), None, None),
        P(("grp", "row")),
    )
    out_specs = (P(("grp", "row"), None), P("row", None))
    return jax.shard_map(shards, mesh=mesh, in_specs=in_specs, out_specs=out_specs, check_vma=False)
```

```python
import functools
import math

import jax
import jax.numpy as jnp
from jax import lax
from jax.experimental import pallas as pl
from jax.experimental.pallas import tpu as pltpu
from jax.sharding import PartitionSpec as P

CONFIDENCE = 40.0
STEPS = 65535.0
OFFSET = 32768
PARTS = 3
BF = jnp.bfloat16
F32 = jnp.float32

VM = pl.BlockSpec(memory_space=pltpu.VMEM)
SM = pl.BlockSpec(memory_space=pltpu.SMEM)
ANY = pl.BlockSpec(memory_space=pl.ANY)
ROWS = (((1,), (1,)), ((), ()))
COLS = (((0,), (0,)), ((), ()))


def call(body, outs, in_specs, flops, moved, scratch=(), mib=24):
    return pl.pallas_call(
        body,
        out_shape=outs,
        in_specs=in_specs,
        out_specs=jax.tree.map(lambda _: VM, outs),
        scratch_shapes=scratch,
        compiler_params=pltpu.CompilerParams(vmem_limit_bytes=mib << 20),
        cost_estimate=pl.CostEstimate(flops=flops, bytes_accessed=moved, transcendentals=0),
    )


def spread_body(n, limit, pair_ref, count_ref, rate_ref, *rest):
    outs, where = rest[: n // 2], rest[n // 2]
    me, (blocks, width, _) = lax.axis_index("row"), rate_ref.shape
    for s in range(n * limit):
        where[s] = -1
    for i in range(blocks):
        @pl.when(i < count_ref[0])
        def _():
            where[pair_ref[1, i]] = i
    for j, out_ref in enumerate(outs):
        for side in range(2):
            for c in range(limit):
                i = where[(me ^ (2 * j + side)) * limit + c]
                rate = rate_ref[jnp.maximum(i, 0)]
                code = jnp.where(i >= 0, (rate * STEPS + 0.5).astype(jnp.int32), 0) - OFFSET
                at = (side * limit + c) * width
                out_ref[at : at + width] = code.astype(jnp.int16)


def halves_body(*refs):
    out_ref = refs[-1]
    for j, ref in enumerate(refs[:-1]):
        rows = ref.shape[0] // 2
        out_ref[j * rows : (j + 1) * rows] = ref[rows:]


def gram_body(item_ref, gram_ref, copy_ref, sem):
    copy = pltpu.make_async_copy(item_ref, copy_ref, sem)
    copy.start()
    copy.wait()
    items = copy_ref[...]
    gram_ref[...] = lax.dot_general(items, items, COLS, preferred_element_type=F32).astype(BF)


def score_body(m, more, item_ref, gram_ref, *rest):
    users, rest = rest[:m], rest[m:]
    total, rest = (rest[0][...], rest[1:]) if more else (None, rest)
    score_ref, user_ref, last_ref, all_ref = rest
    width = users[0].shape[0]
    for j in range(m):
        all_ref[j * width : (j + 1) * width] = users[j][...]
    every = all_ref[...]
    score_ref[...] = lax.dot_general(every, item_ref[...], ROWS, preferred_element_type=F32)
    user_ref[...] = jnp.dot(every, gram_ref[...], preferred_element_type=F32)
    cross = lax.dot_general(every, every, COLS, preferred_element_type=F32)
    if more:
        cross = (total + cross).astype(BF)
        last_ref[...] = jnp.dot(item_ref[...], cross, preferred_element_type=F32)
    else:
        last_ref[...] = cross


def error_body(ks, far, limit, width, send_ref, item_ref, score_refs, gram_refs, users, codes, outs, sum_ref):
    me = lax.axis_index("row")
    for k, user_ref, out_ref in zip(ks, users, outs):
        left = user_ref[...]
        row = k % far
        row = slice(row * width, (row + 1) * width)
        errors, rights, spots = [], [], []
        for c in range(limit):
            at = pl.ds(pl.multiple_of(send_ref[c, me ^ k] * width, width), width)
            code_ref, place = (codes[k], c) if k % 2 == 0 else (codes[1], k // 2 * limit + c)
            code = code_ref[place * width : (place + 1) * width].astype(jnp.int32) + OFFSET
            weighted = CONFIDENCE * (code.astype(F32) * (1.0 / STEPS))
            error = weighted * score_refs[k // far][row, at] - 1.0 - weighted
            errors.append(jnp.where(code > 0, error, 0.0).astype(BF))
            rights.append(item_ref[at])
            spots.append(at)
        error = jnp.concatenate(errors, axis=1)
        total = gram_refs[k // far][row] + jnp.dot(
            error, jnp.concatenate(rights), preferred_element_type=F32
        )
        out_ref[...] = total.astype(out_ref.dtype)
        terms = lax.dot_general(error, left, COLS, preferred_element_type=F32)
        for c, at in enumerate(spots):
            sum_ref[at] += terms[c * width : (c + 1) * width].astype(BF).astype(F32)


def even_body(ks, far, limit, width, send_ref, item_ref, *rest):
    m = len(ks)
    score_refs, gram_refs, part_ref, rest = rest[:2], rest[2:4], rest[4], rest[5:]
    users, codes, outs, sum_ref = rest[:m], rest[m : 2 * m], rest[2 * m : 3 * m], rest[3 * m]
    sum_ref[...] = part_ref[...]
    error_body(
        ks, far, limit, width, send_ref, item_ref, score_refs, gram_refs, users,
        dict(zip(ks, codes)), outs, sum_ref,
    )


def odd_body(ks, far, limit, width, send_ref, item_ref, *rest):
    m = len(ks)
    score_refs, gram_refs, part_ref, rest = rest[:2], rest[2:4], rest[4], rest[5:]
    users, code_ref, rest = rest[:m], rest[m], rest[m + 1 :]
    outs, (mine_ref, other_ref, sum_ref) = rest[:m], rest[m:]
    sum_ref[...] = part_ref[...]
    error_body(
        ks, far, limit, width, send_ref, item_ref, score_refs, gram_refs, users,
        {1: code_ref}, outs, sum_ref,
    )
    core = lax.axis_index("grp") % 2
    half = mine_ref.shape[0]
    other_ref[...] = sum_ref[pl.ds(pl.multiple_of((1 - core) * half, half), half)].astype(BF)
    mine_ref[...] = sum_ref[pl.ds(pl.multiple_of(core * half, half), half)]


def total_body(*refs):
    total = refs[0][...]
    for ref in refs[1:-1]:
        total += ref[...].astype(F32)
    refs[-1][...] = total


def finish_body(user_scale, item_scale, user_ref, total_ref, item_ref, *rest):
    pieces, (users_out, items_out, buf, sems) = rest[:-4], rest[-4:]
    core = lax.axis_index("grp") % 2
    half = pieces[0].shape[0]
    step = half // PARTS
    copies = []
    for side in range(2):
        first = (core + side) % 2 * half
        mine = pieces[side * (len(pieces) // 2) : (side + 1) * (len(pieces) // 2)]
        for i in range(PARTS):
            part = slice(i * step, (i + 1) * step)
            at = pl.ds(pl.multiple_of(first + i * step, step), step)
            total = mine[0][part].astype(F32)
            for piece in mine[1:]:
                total += piece[part].astype(F32)
            buf[at] = item_ref[at].astype(F32) - item_scale * total
            copies.append(
                pltpu.make_async_copy(buf.at[at], items_out.at[at], sems.at[side * PARTS + i])
            )
            copies[-1].start()
    users_out[...] = user_ref[...].astype(F32) - user_scale * total_ref[...]
    for copy in copies:
        copy.wait()


def swap(x, axis, k):
    return lax.ppermute(x, axis, [(i, i ^ k) for i in range(lax.axis_size(axis))])


def shards(users, items, ratings, pair_list, send_list, counts):
    n = lax.axis_size("row")
    grp_n = lax.axis_size("grp")
    width = ratings.shape[2]
    factors = users.shape[1]
    limit = send_list.shape[2]
    item_rows = items.shape[0]
    user_rows = users.shape[0]
    far = n // 2
    hop = n - 2 if n > 2 else 1
    total_users = user_rows * grp_n * n
    total_items = item_rows * n
    sds = jax.ShapeDtypeStruct

    pairs = jnp.swapaxes(pair_list[0], 0, 1)
    sends = jnp.swapaxes(send_list[0], 0, 1)

    over = swap(users, "row", far)
    codes = call(
        functools.partial(spread_body, n, limit),
        [sds((2 * limit * width, width), jnp.int16)] * far,
        [SM, SM, VM],
        0,
        ratings.size * 6,
        [pltpu.SMEM((n * limit,), jnp.int32)],
    )(pairs, counts, ratings[0])
    blocks = [users] + [swap(users, "row", k) for k in range(1, far)]
    blocks[1], *late = lax.optimization_barrier((blocks[1], *codes[1 : far // 2]))
    blocks += [over] + [swap(over, "row", k) for k in range(1, far)]
    along = {j: swap(codes[j], "row", 2 * j) for j in range(far // 2, far)}
    along.update({j: swap(late[j - 1], "row", 2 * j) for j in range(1, far // 2)})
    along = [codes[0]] + [along[j] for j in range(1, far)]
    passed = call(
        halves_body,
        sds((far * limit * width, width), jnp.int16),
        [VM] * far,
        2 * 10**10,
        4 * far * limit * width * width,
    )(*along)

    cross_flops = 2 * user_rows * factors**2
    item_flops = 2 * item_rows * factors**2
    score_flops = 2 * user_rows * factors * item_rows
    gram, rows = call(
        gram_body,
        [sds((factors, factors), BF), sds((item_rows, factors), BF)],
        [ANY],
        item_flops,
        items.size * 4,
        [pltpu.SemaphoreType.DMA],
    )(items)
    score_out = [sds((far * user_rows, item_rows), F32), sds((far * user_rows, factors), F32)]
    every = [pltpu.VMEM((far * user_rows, factors), BF)]
    near_score, near_gram, cross = call(
        functools.partial(score_body, far, False),
        score_out + [sds((factors, factors), F32)],
        [VM] * (2 + far),
        40 * far * (score_flops + 2 * cross_flops),
        4 << 20,
        every,
    )(rows, gram, *blocks[:far])
    far_score, far_gram, item_part = call(
        functools.partial(score_body, far, True),
        score_out + [sds((item_rows, factors), F32)],
        [VM] * (3 + far),
        40 * (far * (score_flops + 2 * cross_flops) + item_flops),
        4 << 20,
        every,
    )(rows, gram, *blocks[far:], cross)
    half = item_rows // 2
    pair_flops = 6 * limit * user_rows * factors * width
    passed = swap(passed, "row", 1)
    scores = (near_score, far_score, near_gram, far_gram)
    evens, odds = range(0, n, 2), [*range(far + 1, n, 2), *range(1, far, 2)]
    *even_terms, sums = call(
        functools.partial(even_body, evens, far, limit, width),
        [sds((user_rows, factors), F32 if k in (0, hop) else BF) for k in evens]
        + [sds((item_rows, factors), F32)],
        [SM] + [VM] * (6 + 2 * len(evens)),
        1 * len(evens) * pair_flops,
        4 << 20,
    )(sends, rows, *scores, item_part, *[blocks[k] for k in evens], *along)
    *odd_terms, mine, other = call(
        functools.partial(odd_body, odds, far, limit, width),
        [sds((user_rows, factors), BF)] * len(odds)
        + [sds((half, factors), F32), sds((half, factors), BF)],
        [SM] + [VM] * (7 + len(odds)),
        0 * len(odds) * pair_flops,
        0,
        [pltpu.VMEM((item_rows, factors), F32)],
    )(sends, rows, *scores, sums, *[blocks[k] for k in odds], passed)
    parts = dict(zip([*evens, *odds], [*even_terms, *odd_terms]))

    across = parts[hop]
    for k in range(1, far):
        across += swap(parts[hop ^ k], "row", k).astype(F32)
    terms = [parts[0], swap(across.astype(BF), "row", hop)]
    terms += [swap(parts[k], "row", k) for k in ((3, 1, 2) if far == 4 else range(1, far))]
    user_sum = call(
        total_body, sds((user_rows, factors), F32), [VM] * len(terms), 5 * 10**9, 16 * user_rows * factors
    )(*terms)

    pair_sum = mine + swap(other, "grp", 1).astype(F32)
    if grp_n == 4:
        here = pair_sum.astype(BF)
        there = swap(here, "grp", 2)
        pieces = [here, there, swap(here, "grp", 1), swap(there, "grp", 1)]
    else:
        peers = [list(range(c, grp_n, 2)) for c in range(2)]
        here = lax.psum(pair_sum, "grp", axis_index_groups=peers)
        pieces = [here, swap(here, "grp", 1)]
    new_users, new_items = pl.pallas_call(
        functools.partial(
            finish_body, 4.0 / math.sqrt(total_items), 8.0 / math.sqrt(total_users)
        ),
        out_shape=[sds((user_rows, factors), F32), sds((item_rows, factors), F32)],
        in_specs=[VM] * (3 + len(pieces)),
        out_specs=[VM, ANY],
        scratch_shapes=[
            pltpu.VMEM((item_rows, factors), F32),
            pltpu.SemaphoreType.DMA((2 * PARTS,)),
        ],
        compiler_params=pltpu.CompilerParams(vmem_limit_bytes=24 << 20),
        cost_estimate=pl.CostEstimate(flops=0, bytes_accessed=4 << 20, transcendentals=0),
    )(users, user_sum, rows, *pieces)
    return (new_users, new_items)


def solution(mesh):
    in_specs = (
        P(("grp", "row"), None),
        P("row", None),
        P(("grp", "row"), None, None, None),
        P(("grp", "row"), None, None),
        P(("grp", "row"), None, None),
        P(("grp", "row")),
    )
    out_specs = (P(("grp", "row"), None), P("row", None))
    return jax.shard_map(shards, mesh=mesh, in_specs=in_specs, out_specs=out_specs, check_vma=False)
```
